32 devices in a mesh: grp: 4 (over x, core), inner: 8 (over z, y).
Axes of the slice: x: 2, y: 2, z: 4, core: 2. Of those that a mesh axis runs over, the one named last changes fastest.
Arguments:
- electric: float32 [3, 16, 128, 512], P(None, None, 'inner', 'grp'), may hold values from -6 to 6
- magnetic: float32 [3, 16, 128, 512], P(None, None, 'inner', 'grp'), may hold values from -6 to 6
- material_ids: int32 [16, 128, 512], P(None, 'inner', 'grp'), may hold values from 0 to 7
- update_ca: float32 [8], replicated, may hold values from 0.6 to 1
- update_cb: float32 [8], replicated, may hold values from 0.12 to 0.45
- face_ranges: int32 [8, 4, 4], P('inner', 'grp'), may hold values from 0 to 128, as said below
- band_table: int32 [32], replicated, may hold values from 0 to 31, each once
Outputs:
- electric_out: float32 [3, 16, 128, 512], P(None, None, 'inner', 'grp')
- magnetic_out: float32 [3, 16, 128, 512], P(None, None, 'inner', 'grp')
- far_field: float32 [32, 8, 128], P(('grp', 'inner'))
The draws below stay inside these ranges and needn't reach their ends.
Inputs may be any that keep to these rules, and one draw needn't show every extreme that they name: `face_ranges`: one box [x0, x1) x [y0, y1) with x0 <= 32, x1 >= 96, y0 <= 128, y1 >= 384 is clipped to each tile: entries are (clip(x0 - i * 16), clip(x1 - i * 16), clip(y0 - j * 128), clip(y1 - j * 128)), each clip into [0, tile width].
All inputs are finite; a program needn't handle non-finite values.
Results may differ from the reference program's by a relative error of at most 0.0003.
Values sent between devices are 32-bit elements; how exact they have to be, the bound alone decides.
A program may use at most 64 MiB of HBM per device.

```python
import math
import jax
import jax.numpy as jnp
from jax import lax

CX = 16
CY = 128
NZ = 16
STEPS = 8
FREQS = 32
ANG_BAND = 4
NMAT = 8
ZF = 8
NX = 128
NY = 512
BANDS = 32


def draw_face_ranges(key, part):
    keys = jax.random.split(key, 4)
    x_low = jax.random.randint(keys[0], (), 0, NX // 4 + 1)
    x_high = jax.random.randint(keys[1], (), NX - NX // 4, NX + 1)
    y_low = jax.random.randint(keys[2], (), 0, NY // 4 + 1)
    y_high = jax.random.randint(keys[3], (), NY - NY // 4, NY + 1)
    start_x = jnp.arange(NX // CX, dtype=jnp.int32) * CX
    start_y = jnp.arange(NY // CY, dtype=jnp.int32) * CY
    low_x = jnp.clip(x_low - start_x, 0, CX)
    high_x = jnp.clip(x_high - start_x, 0, CX)
    low_y = jnp.clip(y_low - start_y, 0, CY)
    high_y = jnp.clip(y_high - start_y, 0, CY)
    grid_shape = (NX // CX, NY // CY)
    return jnp.stack([jnp.broadcast_to(low_x[:, None], grid_shape), jnp.broadcast_to(high_x[:, None], grid_shape), jnp.broadcast_to(low_y[None, :], grid_shape), jnp.broadcast_to(high_y[None, :], grid_shape)], axis=-1).astype(jnp.int32)


def set_ends(drawn, key, least, largest):
    spot = [jax.random.randint(jax.random.fold_in(key, axis), (), 0, length) for axis, length in enumerate(drawn.shape)]
    widest = drawn.shape.index(max(drawn.shape))
    next_to = spot[:widest] + [(spot[widest] + 1) % drawn.shape[widest]] + spot[widest + 1:]
    return drawn.at[tuple(spot)].set(least).at[tuple(next_to)].set(largest)


def steps_of(stream_key, shape, shards, low, high):
    level, own = 1.0, jax.random.fold_in(stream_key, 6)
    for dim, parts in shards:
        heights = jnp.exp(jax.random.uniform(jax.random.fold_in(own, dim), (parts,), jnp.float32, low / len(shards), high / len(shards)))
        level = level * jnp.repeat(heights, shape[dim] // parts).reshape([-1 if axis == dim else 1 for axis in range(len(shape))])
    return level


def normal_values(key, extent, deviation, limit, cuts=(), kind=jnp.bfloat16):
    gain = steps_of(key, extent, cuts, -0.22, 0.18) if cuts else 1.0
    result = jax.random.normal(key, extent, jnp.float32) * deviation * gain
    return jnp.minimum(jnp.maximum(result, -limit), limit).astype(kind)


def setup_inputs(seed: int = 0) -> dict:
    seeds = jax.random.split(jax.random.key(seed), 8)
    electric = normal_values(seeds[0], (3, NZ, NX, NY), 1.0, 6.0, ((2, 8), (3, 4)), jnp.float32)
    magnetic = normal_values(seeds[1], (3, NZ, NX, NY), 1.0, 6.0, ((2, 8), (3, 4)), jnp.float32)
    material_ids = set_ends(jax.random.randint(seeds[2], (NZ, NX, NY), 0, NMAT), jax.random.fold_in(seeds[2], 1), 0, NMAT - 1).astype(jnp.int32)
    update_ca = jnp.clip(jax.random.uniform(seeds[3], (NMAT,), jnp.float32, 0.6, 1.0), 0.6, 1.0)
    update_cb = jnp.clip(jnp.exp(jax.random.uniform(seeds[4], (NMAT,), jnp.float32, math.log(0.12), math.log(0.45))), 0.12, 0.45)
    face_ranges = draw_face_ranges(jax.random.fold_in(seeds[7], 71), 0)
    band_table = jax.random.permutation(seeds[6], BANDS).astype(jnp.int32)
    return {"electric": electric, "magnetic": magnetic, "material_ids": material_ids, "update_ca": update_ca, "update_cb": update_cb, "face_ranges": face_ranges, "band_table": band_table}


def forward_diff(field, axis):
    size = field.shape[axis]
    rest = lax.slice_in_dim(field, 1, size, axis=axis)
    edge = jnp.zeros_like(lax.slice_in_dim(field, 0, 1, axis=axis))
    return jnp.concatenate([rest, edge], axis) - field

def backward_diff(field, axis):
    size = field.shape[axis]
    rest = lax.slice_in_dim(field, 0, size - 1, axis=axis)
    edge = jnp.zeros_like(lax.slice_in_dim(field, 0, 1, axis=axis))
    return field - jnp.concatenate([edge, rest], axis)

def curl_with(field, diff):
    curl_x = diff(field[2], 2) - diff(field[1], 0)
    curl_y = diff(field[0], 0) - diff(field[2], 1)
    curl_z = diff(field[1], 1) - diff(field[0], 2)
    return jnp.stack([curl_x, curl_y, curl_z])

def reference(electric, magnetic, material_ids, update_ca, update_cb, face_ranges, band_table):
    highest = lax.Precision.HIGHEST
    coef_a = update_ca[material_ids]
    coef_b = update_cb[material_ids]
    xcells = jnp.arange(NX, dtype=jnp.int32)
    ycells = jnp.arange(NY, dtype=jnp.int32)
    tile_x = (xcells // CX)[:, None]
    tile_y = (ycells // CY)[None, :]
    local_x = (xcells % CX)[:, None]
    local_y = (ycells % CY)[None, :]
    face_mask = (local_x >= face_ranges[tile_x, tile_y, 0]) & (local_x < face_ranges[tile_x, tile_y, 1]) & (local_y >= face_ranges[tile_x, tile_y, 2]) & (local_y < face_ranges[tile_x, tile_y, 3])
    face_mask = face_mask.astype(jnp.float32)
    recorded = []
    for iteration in range(STEPS):
        magnetic = magnetic - 0.5 * curl_with(electric, forward_diff)
        electric = coef_a * electric + coef_b * curl_with(magnetic, backward_diff)
        recorded.append(jnp.stack([electric[0, ZF], electric[1, ZF], magnetic[0, ZF], magnetic[1, ZF]]) * face_mask)
    samples = jnp.stack(recorded)
    times = jnp.arange(STEPS, dtype=jnp.int32)
    ones_f = jnp.arange(FREQS, dtype=jnp.int32) + 1
    turns = ones_f[:, None] * times[None, :] % 128
    dft_angle = turns.astype(jnp.float32) * jnp.float32(2.0 * math.pi / 128.0)
    dft_cos = jnp.cos(dft_angle)
    dft_sin = jnp.sin(dft_angle)
    b_dirs = jnp.arange(ANG_BAND, dtype=jnp.int32) * 33 // ANG_BAND - 16
    a_dirs = band_table.astype(jnp.int32) - BANDS // 2
    scale = 1.0 / math.sqrt(NX * NY)

    def one_freq(freq_idx):
        mult = freq_idx + 1
        cur_re = jnp.einsum('n,ncxy->cxy', dft_cos[freq_idx], samples, precision=highest)
        cur_im = -jnp.einsum('n,ncxy->cxy', dft_sin[freq_idx], samples, precision=highest)
        turn_y = mult * ycells[:, None] * b_dirs[None, :] % 4096
        ang_y = turn_y.astype(jnp.float32) * jnp.float32(2.0 * math.pi / 4096.0)
        cos_y = jnp.cos(ang_y)
        sin_y = jnp.sin(ang_y)
        col_re = jnp.einsum('cxy,yq->cxq', cur_re, cos_y, precision=highest) - jnp.einsum('cxy,yq->cxq', cur_im, sin_y, precision=highest)
        col_im = jnp.einsum('cxy,yq->cxq', cur_re, sin_y, precision=highest) + jnp.einsum('cxy,yq->cxq', cur_im, cos_y, precision=highest)
        turn_x = mult * a_dirs[:, None] * xcells[None, :] % 4096
        ang_x = turn_x.astype(jnp.float32) * jnp.float32(2.0 * math.pi / 4096.0)
        cos_x = jnp.cos(ang_x)
        sin_x = jnp.sin(ang_x)
        far_re = jnp.einsum('px,cxq->pcq', cos_x, col_re, precision=highest) - jnp.einsum('px,cxq->pcq', sin_x, col_im, precision=highest)
        far_im = jnp.einsum('px,cxq->pcq', sin_x, col_re, precision=highest) + jnp.einsum('px,cxq->pcq', cos_x, col_im, precision=highest)
        return (far_re, far_im)
    far_re, far_im = lax.map(one_freq, jnp.arange(FREQS, dtype=jnp.int32))
    joined = jnp.concatenate([far_re, far_im], axis=2)
    joined = jnp.transpose(joined, (1, 2, 3, 0)).reshape(BANDS, 8, ANG_BAND * FREQS)
    return (electric, magnetic, joined * scale)
```

```python
import functools
import math

import jax
import jax.numpy as jnp
import numpy as np
from jax import lax
from jax.experimental import pallas as pl
from jax.experimental.pallas import tpu as pltpu
from jax.sharding import PartitionSpec as P

STEPS = 8
FREQS = 32
ANG_BAND = 4
NMAT = 8
ZF = 8
NZ = 16
CX = 16
CY = 128
PITCH = 24
BASE = 8
MESH = pl.DeviceIdType.MESH


def tables(bands, groups):
    f = np.tile(np.arange(FREQS, dtype=np.int64) + 1, ANG_BAND)
    b = np.repeat(np.arange(ANG_BAND, dtype=np.int64) * 33 // ANG_BAND - 16, FREQS)
    a = np.arange(bands, dtype=np.int64) - bands // 2

    def both(turns, period):
        angle = (turns % period) * (2.0 * math.pi / period)
        return np.cos(angle).astype(np.float32), np.sin(angle).astype(np.float32)

    y = np.arange(CY, dtype=np.int64)[:, None]
    proj = np.concatenate(both(f * b * y, 4096), axis=1)
    time = np.stack(both(f * np.arange(STEPS, dtype=np.int64)[:, None], 128))
    y_start = np.stack(both(f * b * CY * np.arange(groups, dtype=np.int64)[:, None], 4096))
    cell = np.stack(both(f * a[:, None], 4096))
    block = np.stack(both(f * a[:, None] * CX, 4096))
    return proj, time, y_start, cell, block


def kernel(
    ny, nx, scale,
    e_in, h_in, ids, ca, cb, face, bands, proj, time, y_start, cell, block,
    e_out, h_out, far_out,
    ep, hp, coef_a, coef_b,
    xs_r, xs_l, ys_r, ys_l, xr_l, xr_r, yr_l, yr_r, cor_x, cor_y,
    sample, acc, cols, phase, f_send, f_recv,
    send_sem, recv_sem, f_send_sem, f_recv_sem,
):
    iy = lax.axis_index("grp")
    ix = lax.axis_index("inner")
    total = ny * nx
    me = iy * nx + ix
    lane = lax.broadcasted_iota(jnp.int32, (CX, CY), 1)
    row = lax.broadcasted_iota(jnp.int32, (CX, CY), 0)

    for buf in (xr_l, xr_r, yr_l, yr_r, cor_x, cor_y):
        buf[...] = jnp.zeros(buf.shape, jnp.float32)

    barrier = pltpu.get_barrier_semaphore()

    def greet(k, carry):
        other = lax.rem(me + k, total)
        pl.semaphore_signal(
            barrier, inc=1, device_id=(lax.div(other, nx), lax.rem(other, nx)), device_id_type=MESH
        )
        return carry

    lax.fori_loop(1, total, greet, 0)

    def at(z, shift=0):
        return pl.ds(z * PITCH + BASE + shift, CX)

    def plane(x):
        return pl.ds(BASE + x, NZ, stride=PITCH)

    for c in range(3):
        for z in range(NZ):
            ep[c, at(z), :] = e_in[c, pl.ds(z * CX, CX), :]
            hp[c, at(z), :] = h_in[c, pl.ds(z * CX, CX), :]
    for z in range(NZ):
        here = ids[pl.ds(z * CX, CX), :]
        va = jnp.zeros((CX, CY), jnp.float32)
        vb = jnp.zeros((CX, CY), jnp.float32)
        for m in range(NMAT):
            chosen = here == m
            va = jnp.where(chosen, ca[m], va)
            vb = jnp.where(chosen, cb[m], vb)
        coef_a[pl.ds(z * CX, CX), :] = va
        coef_b[pl.ds(z * CX, CX), :] = vb
    sample[...] = jnp.zeros(sample.shape, jnp.float32)
    acc[...] = jnp.zeros(acc.shape, jnp.float32)
    on_face = (row >= face[0]) & (row < face[1]) & (lane >= face[2]) & (lane < face[3])
    inside_x = jnp.where(ix > 0, 1.0, 0.0).astype(jnp.float32)
    inside_y = jnp.where(iy > 0, 1.0, 0.0).astype(jnp.float32)

    def power(bit, carry):
        pr, pi, br, bi = carry
        take = lax.rem(lax.shift_right_logical(ix, bit), 2) == 1
        nr = pr * br - pi * bi
        ni = pr * bi + pi * br
        return (
            jnp.where(take, nr, pr),
            jnp.where(take, ni, pi),
            br * br - bi * bi,
            2.0 * br * bi,
        )

    rows_at_once = 8
    for start in range(0, total, rows_at_once):
        part = pl.ds(start, rows_at_once)
        carry = (
            jnp.full((rows_at_once, CY), scale, jnp.float32),
            jnp.zeros((rows_at_once, CY), jnp.float32),
            block[0, part, :],
            block[1, part, :],
        )
        for bit in range(max(1, (nx - 1).bit_length())):
            carry = power(bit, carry)
        phase[0, part, :] = carry[0]
        phase[1, part, :] = carry[1]

    pl.semaphore_wait(barrier, total - 1)

    has_xr, has_xl = ix < nx - 1, ix > 0
    has_yr, has_yl = iy < ny - 1, iy > 0

    def copies(n):
        return (
            (has_xr, has_xl, xs_r.at[n], xr_l.at[n], (iy, ix + 1)),
            (has_xl, has_xr, xs_l.at[n], xr_r.at[n], (iy, ix - 1)),
            (has_yr, has_yl, ys_r.at[n], yr_l.at[n], (iy + 1, ix)),
            (has_yl, has_yr, ys_l.at[n], yr_r.at[n], (iy - 1, ix)),
            (has_xr & has_yl, has_xl & has_yr, xs_r.at[n, pl.ds(0, NZ)], cor_x.at[n], (iy - 1, ix + 1)),
            (has_xl & has_yr, has_xr & has_yl, ys_r.at[n, pl.ds(0, 8)], cor_y.at[n], (iy + 1, ix - 1)),
        )

    def remote(n, i, src, dst, device):
        return pltpu.make_async_remote_copy(
            src_ref=src,
            dst_ref=dst,
            send_sem=send_sem.at[i],
            recv_sem=recv_sem.at[n, i],
            device_id=device,
            device_id_type=MESH,
        )

    def add_sample(n):
        g = jnp.dot(
            sample[...], proj[...], precision=lax.Precision.HIGHEST, preferred_element_type=jnp.float32
        )
        g_re, g_im = g[:, :CY], g[:, CY:]
        ct = time[0, pl.ds(n, 1), :]
        st = time[1, pl.ds(n, 1), :]
        acc[0] += ct * g_re + st * g_im
        acc[1] += ct * g_im - st * g_re

    def step(n, carry):
        last = jnp.zeros((CX, CY), jnp.float32)
        first = jnp.zeros((CX, CY), jnp.float32)
        for g, (field, c) in enumerate(((ep, 0), (ep, 1), (ep, 2), (hp, 1), (hp, 2))):
            xs_r[n, pl.ds(g * NZ, NZ), :] = field[c, plane(CX - 1), :]
        for g, c in enumerate((1, 2)):
            xs_l[n, pl.ds(g * NZ, NZ), :] = ep[c, plane(0), :]
        for z in range(NZ):
            for g, (field, c) in enumerate(((ep, 0), (ep, 1), (ep, 2), (hp, 0), (hp, 2))):
                spot = g * NZ + z
                last = jnp.where(lane == spot, pltpu.roll(field[c, at(z), :], (spot - CY + 1) % CY, 1), last)
            for g, c in enumerate((0, 2)):
                spot = g * NZ + z
                value = ep[c, at(z), :]
                first = jnp.where(lane == spot, pltpu.roll(value, spot, 1) if spot else value, first)
        ys_r[n] = last
        ys_l[n] = first
        for i, (sends, _, src, dst, device) in enumerate(copies(n)):
            @pl.when(sends)
            def _(i=i, src=src, dst=dst, device=device):
                remote(n, i, src, dst, device).start()

        add_sample(jnp.maximum(n - 1, 0))

        for i, (_, receives, src, dst, _) in enumerate(copies(n)):
            @pl.when(receives)
            def _(i=i, src=src, dst=dst):
                remote(n, i, src, dst, (iy, ix)).wait_recv()

        ex, ey, ez, hy, hz = (xr_l[n, pl.ds(g * NZ, NZ), :] for g in range(5))
        ey0, ez0 = xs_l[n, pl.ds(0, NZ), :], xs_l[n, pl.ds(NZ, NZ), :]
        ep[1, plane(CX), :] = xr_r[n, pl.ds(0, NZ), :]
        ep[2, plane(CX), :] = xr_r[n, pl.ds(NZ, NZ), :]
        ex_z = jnp.where(row == NZ - 1, 0.0, pltpu.roll(ex, NZ - 1, 0))
        ex_y = pltpu.roll(jnp.where(lane == 0, cor_x[n], ex), CY - 1, 1)
        hp[1, plane(-1), :] = inside_x * (hy - 0.5 * ((ex_z - ex) - (ez0 - ez)))
        hp[2, plane(-1), :] = inside_x * (hz - 0.5 * ((ey0 - ey) - (ex_y - ex)))

        packed, own = yr_l[n], ys_l[n]
        ex = packed
        ey, ez, hx, hz = (pltpu.roll(packed, CY - g * NZ, 1) for g in range(1, 5))
        ex0, ez0 = own, pltpu.roll(own, CY - NZ, 1)
        ey_z = jnp.where(lane == NZ - 1, 0.0, pltpu.roll(ey, CY - 1, 1))
        corner = pltpu.roll(cor_y[n], CY - NZ, 1)[0:1, :]
        ey_x = jnp.where(row == CX - 1, corner, pltpu.roll(ey, CX - 1, 0))
        hx_col = inside_y * (hx - 0.5 * ((ez0 - ez) - (ey_z - ey)))
        hz_col = inside_y * (hz - 0.5 * ((ey_x - ey) - (ex0 - ex)))

        after = yr_r[n]
        zero = jnp.zeros((CX, CY), jnp.float32)
        for z in range(NZ):
            ex, ey, ez = (ep[c, at(z), :] for c in range(3))
            ex_z = ep[0, at(z + 1), :] if z < NZ - 1 else zero
            ey_z = ep[1, at(z + 1), :] if z < NZ - 1 else zero
            ey_x = ep[1, at(z, 1), :]
            ez_x = ep[2, at(z, 1), :]
            ex_y = jnp.where(
                lane == CY - 1, pltpu.roll(after, CY - 1 - z, 1), pltpu.roll(ex, CY - 1, 1)
            )
            ez_y = jnp.where(
                lane == CY - 1, pltpu.roll(after, CY - 1 - NZ - z, 1), pltpu.roll(ez, CY - 1, 1)
            )
            hp[0, at(z), :] = hp[0, at(z), :] - 0.5 * ((ez_y - ez) - (ey_z - ey))
            hp[1, at(z), :] = hp[1, at(z), :] - 0.5 * ((ex_z - ex) - (ez_x - ez))
            hp[2, at(z), :] = hp[2, at(z), :] - 0.5 * ((ey_x - ey) - (ex_y - ex))
        for z in range(NZ):
            hx, hy, hz = (hp[c, at(z), :] for c in range(3))
            hx_z = hp[0, at(z - 1), :] if z else zero
            hy_z = hp[1, at(z - 1), :] if z else zero
            hy_x = hp[1, at(z, -1), :]
            hz_x = hp[2, at(z, -1), :]
            hx_y = jnp.where(lane == 0, pltpu.roll(hx_col, CY - z, 1) if z else hx_col, pltpu.roll(hx, 1, 1))
            hz_y = jnp.where(lane == 0, pltpu.roll(hz_col, CY - z, 1) if z else hz_col, pltpu.roll(hz, 1, 1))
            va, vb = coef_a[pl.ds(z * CX, CX), :], coef_b[pl.ds(z * CX, CX), :]
            ex = va * ep[0, at(z), :] + vb * ((hz - hz_y) - (hy - hy_z))
            ey = va * ep[1, at(z), :] + vb * ((hx - hx_z) - (hz - hz_x))
            ep[0, at(z), :] = ex
            ep[1, at(z), :] = ey
            ep[2, at(z), :] = va * ep[2, at(z), :] + vb * ((hy - hy_x) - (hx - hx_y))
            if z == ZF:
                for c, value in enumerate((ex, ey, hx, hy)):
                    sample[pl.ds(c * CX, CX), :] = jnp.where(on_face, value, 0.0)

        for i, (sends, _, src, dst, device) in enumerate(copies(n)):
            @pl.when(sends)
            def _(i=i, src=src, dst=dst, device=device):
                remote(n, i, src, dst, device).wait_send()
        return carry

    lax.fori_loop(0, STEPS, step, 0)
    add_sample(STEPS - 1)

    yr = y_start[0, pl.ds(iy, 1), :]
    yi = y_start[1, pl.ds(iy, 1), :]
    col_re = acc[0] * yr - acc[1] * yi
    acc[1] = acc[0] * yi + acc[1] * yr
    acc[0] = col_re
    for part in range(2):
        for x in range(CX):
            four = acc[part, pl.ds(x, 4, stride=CX), :]
            cols[part, x, pl.ds(0, 4), :] = four
            cols[part, x, pl.ds(4, 4), :] = four

    upper = lax.broadcasted_iota(jnp.int32, (8, CY), 0) < 4
    at_once = min(8, total)

    def send_far(k):
        other = lax.rem(me + k, total)
        return pltpu.make_async_remote_copy(
            src_ref=f_send.at[k],
            dst_ref=f_recv.at[k - 1],
            send_sem=f_send_sem,
            recv_sem=f_recv_sem,
            device_id=(lax.div(other, nx), lax.rem(other, nx)),
            device_id_type=MESH,
        )

    def project(trip, carry):
        k0 = trip * at_once
        picked = [bands[lax.rem(me + k0 + j, total)] for j in range(at_once)]

        def pair(table, part, j):
            return jnp.where(
                upper, table[part, pl.ds(picked[j], 1), :], table[part, pl.ds(picked[j + 1], 1), :]
            )

        pairs = range(0, at_once, 2)
        wr = [pair(cell, 0, j) for j in pairs]
        wi = [pair(cell, 1, j) for j in pairs]
        c_re, c_im = cols[0, CX - 1], cols[1, CX - 1]
        re = [c_re for _ in pairs]
        im = [c_im for _ in pairs]
        for x in range(CX - 2, -1, -1):
            c_re, c_im = cols[0, x], cols[1, x]
            re, im = (
                [r * a - i * b + c_re for r, i, a, b in zip(re, im, wr, wi)],
                [r * b + i * a + c_im for r, i, a, b in zip(re, im, wr, wi)],
            )
        for t, j in enumerate(pairs):
            pr, pi = pair(phase, 0, j), pair(phase, 1, j)
            far_re = re[t] * pr - im[t] * pi
            far_im = re[t] * pi + im[t] * pr
            f_send[k0 + j] = jnp.where(upper, far_re, pltpu.roll(far_im, 4, 0))
            f_send[k0 + j + 1] = jnp.where(upper, pltpu.roll(far_re, 4, 0), far_im)
        for j in range(at_once):
            @pl.when(k0 + j > 0)
            def _(j=j):
                send_far(k0 + j).start()
        return carry

    lax.fori_loop(0, total // at_once, project, 0)

    for c in range(3):
        for z in range(NZ):
            e_out[c, pl.ds(z * CX, CX), :] = ep[c, at(z), :]
            h_out[c, pl.ds(z * CX, CX), :] = hp[c, at(z), :]

    pltpu.make_async_copy(f_recv, f_recv, f_recv_sem).wait()
    if total <= 64:
        terms = [f_send[0]] + [f_recv[k] for k in range(total - 1)]
        while len(terms) > 1:
            terms = [a + b for a, b in zip(terms[::2], terms[1::2])]
        far_out[...] = terms[0]
    else:
        far_out[...] = lax.fori_loop(0, total - 1, lambda k, t: t + f_recv[k], f_send[0])
    pltpu.make_async_copy(f_recv, f_recv, f_send_sem).wait()


def local(ny, nx, electric, magnetic, material_ids, update_ca, update_cb, face_ranges, band_table):
    total = ny * nx
    bands = band_table.shape[0]
    assert bands == total and electric.shape == (3, NZ, CX, CY)
    scale = 1.0 / math.sqrt(CX * nx * CY * ny)
    f32 = jnp.float32
    vmem = pl.BlockSpec(memory_space=pltpu.VMEM)
    smem = pl.BlockSpec(memory_space=pltpu.SMEM)
    rows = NZ * CX
    e_out, h_out, far = pl.pallas_call(
        functools.partial(kernel, ny, nx, scale),
        out_shape=(
            jax.ShapeDtypeStruct((3, rows, CY), f32),
            jax.ShapeDtypeStruct((3, rows, CY), f32),
            jax.ShapeDtypeStruct((8, CY), f32),
        ),
        in_specs=[vmem] * 3 + [smem] * 4 + [vmem] * 5,
        out_specs=(vmem, vmem, vmem),
        scratch_shapes=[
            pltpu.VMEM((3, NZ * PITCH + 8, CY), f32),
            pltpu.VMEM((3, NZ * PITCH + 8, CY), f32),
            pltpu.VMEM((rows, CY), f32),
            pltpu.VMEM((rows, CY), f32),
            pltpu.VMEM((STEPS, 5 * NZ, CY), f32),
            pltpu.VMEM((STEPS, 2 * NZ, CY), f32),
            pltpu.VMEM((STEPS, CX, CY), f32),
            pltpu.VMEM((STEPS, CX, CY), f32),
            pltpu.VMEM((STEPS, 5 * NZ, CY), f32),
            pltpu.VMEM((STEPS, 2 * NZ, CY), f32),
            pltpu.VMEM((STEPS, CX, CY), f32),
            pltpu.VMEM((STEPS, CX, CY), f32),
            pltpu.VMEM((STEPS, NZ, CY), f32),
            pltpu.VMEM((STEPS, 8, CY), f32),
            pltpu.VMEM((4 * CX, CY), f32),
            pltpu.VMEM((2, 4 * CX, CY), f32),
            pltpu.VMEM((2, CX, 8, CY), f32),
            pltpu.VMEM((2, total, CY), f32),
            pltpu.VMEM((total, 8, CY), f32),
            pltpu.VMEM((total - 1, 8, CY), f32),
            pltpu.SemaphoreType.DMA((6,)),
            pltpu.SemaphoreType.DMA((STEPS, 6)),
            pltpu.SemaphoreType.DMA,
            pltpu.SemaphoreType.DMA,
        ],
        compiler_params=pltpu.CompilerParams(
            collective_id=0, has_side_effects=True, vmem_limit_bytes=32 * 1024 * 1024
        ),
        name="fdtd",
    )(
        electric.reshape(3, rows, CY),
        magnetic.reshape(3, rows, CY),
        material_ids.reshape(rows, CY),
        update_ca,
        update_cb,
        face_ranges.reshape(4),
        band_table,
        *tables(bands, ny),
    )
    return (
        e_out.reshape(electric.shape),
        h_out.reshape(electric.shape),
        far.reshape(1, 8, CY),
    )


def solution(mesh):
    in_specs = (
        P(None, None, "inner", "grp"),
        P(None, None, "inner", "grp"),
        P(None, "inner", "grp"),
        P(),
        P(),
        P("inner", "grp", None),
        P(),
    )
    out_specs = (
        P(None, None, "inner", "grp"),
        P(None, None, "inner", "grp"),
        P(("grp", "inner"), None, None),
    )
    body = functools.partial(local, mesh.shape["grp"], mesh.shape["inner"])
    return jax.shard_map(body, mesh=mesh, in_specs=in_specs, out_specs=out_specs, check_vma=False)
```

```python
import functools
import math

import jax
import jax.numpy as jnp
import numpy as np
from jax import lax
from jax.experimental import pallas as pl
from jax.experimental.pallas import tpu as pltpu
from jax.sharding import PartitionSpec as P

STEPS = 8
FREQS = 32
ANG_BAND = 4
NMAT = 8
ZF = 8
NZ = 16
CX = 16
CY = 128
PITCH = 24
BASE = 8
MESH = pl.DeviceIdType.MESH


def tables(bands, groups):
    f = np.tile(np.arange(FREQS, dtype=np.int64) + 1, ANG_BAND)
    b = np.repeat(np.arange(ANG_BAND, dtype=np.int64) * 33 // ANG_BAND - 16, FREQS)
    a = np.arange(bands, dtype=np.int64) - bands // 2

    def both(turns, period):
        angle = (turns % period) * (2.0 * math.pi / period)
        return np.cos(angle).astype(np.float32), np.sin(angle).astype(np.float32)

    y = np.arange(CY, dtype=np.int64)[:, None]
    proj = np.concatenate(both(f * b * y, 4096), axis=1)
    time = np.stack(both(f * np.arange(STEPS, dtype=np.int64)[:, None], 128))
    y_start = np.stack(both(f * b * CY * np.arange(groups, dtype=np.int64)[:, None], 4096))
    cell = np.stack(both(f * a[:, None], 4096))
    block = np.stack(both(f * a[:, None] * CX, 4096))
    flat = [proj[:, :CY], proj[:, CY:]] + [part for table in (time, y_start, cell, block) for part in table]
    starts = np.cumsum([0] + [-(-part.shape[0] // 8) * 8 for part in flat])
    packed = np.zeros((starts[-1], CY), np.float32)
    for start, part in zip(starts, flat):
        packed[start : start + part.shape[0]] = part
    return packed, tuple(int(start) for start in starts[:-1])


class Rows:
    def __init__(self, ref, starts):
        self.ref, self.starts = ref, starts

    def at(self, part, first, count):
        return self.ref[pl.ds(self.starts[part] + first, count), :]


def kernel(
    ny, nx, scale, starts,
    e_hbm, h_hbm, ids_hbm, ca_hbm, cb_hbm, face_hbm, bands_hbm, table_hbm,
    e_out, h_out, far_out,
    e_in, h_in, ids, ca, cb, face, bands, table, in_sem,
    ep, hp, coef_a, coef_b,
    xs_r, xs_l, ys_r, ys_l, xr_l, xr_r, yr_l, yr_r, cor_x, cor_y,
    sample, acc, cols, phase, f_send, f_recv,
    send_sem, recv_sem, f_send_sem, f_recv_sem,
):
    iy = lax.axis_index("grp")
    ix = lax.axis_index("inner")
    total = ny * nx
    me = iy * nx + ix
    lane = lax.broadcasted_iota(jnp.int32, (CX, CY), 1)
    row = lax.broadcasted_iota(jnp.int32, (CX, CY), 0)

    loads = [
        pltpu.make_async_copy(src, dst, in_sem.at[i])
        for i, (src, dst) in enumerate(
            (
                (e_hbm, e_in),
                (h_hbm, h_in),
                (ids_hbm, ids),
                (ca_hbm, ca),
                (cb_hbm, cb),
                (face_hbm, face),
                (bands_hbm, bands),
                (table_hbm, table),
            )
        )
    ]
    for load in loads:
        load.start()
    time, y_start, cell, block = (Rows(table, starts[i : i + 2]) for i in (2, 4, 6, 8))

    for buf in (xr_l, xr_r, yr_l, yr_r, cor_x, cor_y):
        buf[...] = jnp.zeros(buf.shape, jnp.float32)

    barrier = pltpu.get_barrier_semaphore()

    def greet(k, carry):
        other = lax.rem(me + k, total)
        pl.semaphore_signal(
            barrier, inc=1, device_id=(lax.div(other, nx), lax.rem(other, nx)), device_id_type=MESH
        )
        return carry

    lax.fori_loop(1, total, greet, 0)

    def at(z, shift=0):
        return pl.ds(z * PITCH + BASE + shift, CX)

    def plane(x):
        return pl.ds(BASE + x, NZ, stride=PITCH)

    for load in loads:
        load.wait()
    for c in range(3):
        for z in range(NZ):
            ep[c, at(z), :] = e_in[c, pl.ds(z * CX, CX), :]
            hp[c, at(z), :] = h_in[c, pl.ds(z * CX, CX), :]
    for z in range(NZ):
        here = ids[pl.ds(z * CX, CX), :]
        va = jnp.zeros((CX, CY), jnp.float32)
        vb = jnp.zeros((CX, CY), jnp.float32)
        for m in range(NMAT):
            chosen = here == m
            va = jnp.where(chosen, ca[m], va)
            vb = jnp.where(chosen, cb[m], vb)
        coef_a[pl.ds(z * CX, CX), :] = va
        coef_b[pl.ds(z * CX, CX), :] = vb
    sample[...] = jnp.zeros(sample.shape, jnp.float32)
    acc[...] = jnp.zeros(acc.shape, jnp.float32)
    on_face = (row >= face[0]) & (row < face[1]) & (lane >= face[2]) & (lane < face[3])
    inside_x = jnp.where(ix > 0, 1.0, 0.0).astype(jnp.float32)
    inside_y = jnp.where(iy > 0, 1.0, 0.0).astype(jnp.float32)

    def power(bit, carry):
        pr, pi, br, bi = carry
        take = lax.rem(lax.shift_right_logical(ix, bit), 2) == 1
        nr = pr * br - pi * bi
        ni = pr * bi + pi * br
        return (
            jnp.where(take, nr, pr),
            jnp.where(take, ni, pi),
            br * br - bi * bi,
            2.0 * br * bi,
        )

    rows_at_once = 8
    for start in range(0, total, rows_at_once):
        part = pl.ds(start, rows_at_once)
        carry = (
            jnp.full((rows_at_once, CY), scale, jnp.float32),
            jnp.zeros((rows_at_once, CY), jnp.float32),
            block.at(0, start, rows_at_once),
            block.at(1, start, rows_at_once),
        )
        for bit in range(max(1, (nx - 1).bit_length())):
            carry = power(bit, carry)
        phase[part, :] = carry[0]
        phase[pl.ds(total + start, rows_at_once), :] = carry[1]

    start_phase = Rows(phase, (0, total))
    pl.semaphore_wait(barrier, total - 1)

    has_xr, has_xl = ix < nx - 1, ix > 0
    has_yr, has_yl = iy < ny - 1, iy > 0

    def copies(n):
        return (
            (has_xr, has_xl, xs_r.at[n], xr_l.at[n], (iy, ix + 1)),
            (has_xl, has_xr, xs_l.at[n], xr_r.at[n], (iy, ix - 1)),
            (has_yr, has_yl, ys_r.at[n], yr_l.at[n], (iy + 1, ix)),
            (has_yl, has_yr, ys_l.at[n], yr_r.at[n], (iy - 1, ix)),
            (has_xr & has_yl, has_xl & has_yr, xs_r.at[n, pl.ds(0, NZ)], cor_x.at[n], (iy - 1, ix + 1)),
            (has_xl & has_yr, has_xr & has_yl, ys_r.at[n, pl.ds(0, 8)], cor_y.at[n], (iy + 1, ix - 1)),
        )

    def remote(n, i, src, dst, device):
        return pltpu.make_async_remote_copy(
            src_ref=src,
            dst_ref=dst,
            send_sem=send_sem.at[i],
            recv_sem=recv_sem.at[n, i],
            device_id=device,
            device_id_type=MESH,
        )

    def add_sample(n):
        g_re, g_im = (
            jnp.dot(
                sample[...],
                table[pl.ds(starts[part], CY), :],
                precision=lax.Precision.HIGHEST,
                preferred_element_type=jnp.float32,
            )
            for part in range(2)
        )
        ct, st = time.at(0, n, 1), time.at(1, n, 1)
        acc[0] += ct * g_re + st * g_im
        acc[1] += ct * g_im - st * g_re

    def step(n, carry):
        last = jnp.zeros((CX, CY), jnp.float32)
        first = jnp.zeros((CX, CY), jnp.float32)
        for g, (field, c) in enumerate(((ep, 0), (ep, 1), (ep, 2), (hp, 1), (hp, 2))):
            xs_r[n, pl.ds(g * NZ, NZ), :] = field[c, plane(CX - 1), :]
        for g, c in enumerate((1, 2)):
            xs_l[n, pl.ds(g * NZ, NZ), :] = ep[c, plane(0), :]
        for z in range(NZ):
            for g, (field, c) in enumerate(((ep, 0), (ep, 1), (ep, 2), (hp, 0), (hp, 2))):
                spot = g * NZ + z
                last = jnp.where(lane == spot, pltpu.roll(field[c, at(z), :], (spot - CY + 1) % CY, 1), last)
            for g, c in enumerate((0, 2)):
                spot = g * NZ + z
                value = ep[c, at(z), :]
                first = jnp.where(lane == spot, pltpu.roll(value, spot, 1) if spot else value, first)
        ys_r[n] = last
        ys_l[n] = first
        for i, (sends, _, src, dst, device) in enumerate(copies(n)):
            @pl.when(sends)
            def _(i=i, src=src, dst=dst, device=device):
                remote(n, i, src, dst, device).start()

        add_sample(jnp.maximum(n - 1, 0))

        for i, (_, receives, src, dst, _) in enumerate(copies(n)):
            @pl.when(receives)
            def _(i=i, src=src, dst=dst):
                remote(n, i, src, dst, (iy, ix)).wait_recv()

        ex, ey, ez, hy, hz = (xr_l[n, pl.ds(g * NZ, NZ), :] for g in range(5))
        ey0, ez0 = xs_l[n, pl.ds(0, NZ), :], xs_l[n, pl.ds(NZ, NZ), :]
        ep[1, plane(CX), :] = xr_r[n, pl.ds(0, NZ), :]
        ep[2, plane(CX), :] = xr_r[n, pl.ds(NZ, NZ), :]
        ex_z = jnp.where(row == NZ - 1, 0.0, pltpu.roll(ex, NZ - 1, 0))
        ex_y = pltpu.roll(jnp.where(lane == 0, cor_x[n], ex), CY - 1, 1)
        hp[1, plane(-1), :] = inside_x * (hy - 0.5 * ((ex_z - ex) - (ez0 - ez)))
        hp[2, plane(-1), :] = inside_x * (hz - 0.5 * ((ey0 - ey) - (ex_y - ex)))

        packed, own = yr_l[n], ys_l[n]
        ex = packed
        ey, ez, hx, hz = (pltpu.roll(packed, CY - g * NZ, 1) for g in range(1, 5))
        ex0, ez0 = own, pltpu.roll(own, CY - NZ, 1)
        ey_z = jnp.where(lane == NZ - 1, 0.0, pltpu.roll(ey, CY - 1, 1))
        corner = pltpu.roll(cor_y[n], CY - NZ, 1)[0:1, :]
        ey_x = jnp.where(row == CX - 1, corner, pltpu.roll(ey, CX - 1, 0))
        hx_col = inside_y * (hx - 0.5 * ((ez0 - ez) - (ey_z - ey)))
        hz_col = inside_y * (hz - 0.5 * ((ey_x - ey) - (ex0 - ex)))

        after = yr_r[n]
        zero = jnp.zeros((CX, CY), jnp.float32)
        for z in range(NZ):
            ex, ey, ez = (ep[c, at(z), :] for c in range(3))
            ex_z = ep[0, at(z + 1), :] if z < NZ - 1 else zero
            ey_z = ep[1, at(z + 1), :] if z < NZ - 1 else zero
            ey_x = ep[1, at(z, 1), :]
            ez_x = ep[2, at(z, 1), :]
            ex_y = jnp.where(
                lane == CY - 1, pltpu.roll(after, CY - 1 - z, 1), pltpu.roll(ex, CY - 1, 1)
            )
            ez_y = jnp.where(
                lane == CY - 1, pltpu.roll(after, CY - 1 - NZ - z, 1), pltpu.roll(ez, CY - 1, 1)
            )
            hp[0, at(z), :] = hp[0, at(z), :] - 0.5 * ((ez_y - ez) - (ey_z - ey))
            hp[1, at(z), :] = hp[1, at(z), :] - 0.5 * ((ex_z - ex) - (ez_x - ez))
            hp[2, at(z), :] = hp[2, at(z), :] - 0.5 * ((ey_x - ey) - (ex_y - ex))
        for z in range(NZ):
            hx, hy, hz = (hp[c, at(z), :] for c in range(3))
            hx_z = hp[0, at(z - 1), :] if z else zero
            hy_z = hp[1, at(z - 1), :] if z else zero
            hy_x = hp[1, at(z, -1), :]
            hz_x = hp[2, at(z, -1), :]
            hx_y = jnp.where(lane == 0, pltpu.roll(hx_col, CY - z, 1) if z else hx_col, pltpu.roll(hx, 1, 1))
            hz_y = jnp.where(lane == 0, pltpu.roll(hz_col, CY - z, 1) if z else hz_col, pltpu.roll(hz, 1, 1))
            va, vb = coef_a[pl.ds(z * CX, CX), :], coef_b[pl.ds(z * CX, CX), :]
            ex = va * ep[0, at(z), :] + vb * ((hz - hz_y) - (hy - hy_z))
            ey = va * ep[1, at(z), :] + vb * ((hx - hx_z) - (hz - hz_x))
            ep[0, at(z), :] = ex
            ep[1, at(z), :] = ey
            ep[2, at(z), :] = va * ep[2, at(z), :] + vb * ((hy - hy_x) - (hx - hx_y))
            if z == ZF:
                for c, value in enumerate((ex, ey, hx, hy)):
                    sample[pl.ds(c * CX, CX), :] = jnp.where(on_face, value, 0.0)

        for i, (sends, _, src, dst, device) in enumerate(copies(n)):
            @pl.when(sends)
            def _(i=i, src=src, dst=dst, device=device):
                remote(n, i, src, dst, device).wait_send()
        return carry

    lax.fori_loop(0, STEPS, step, 0)
    add_sample(STEPS - 1)

    yr, yi = y_start.at(0, iy, 1), y_start.at(1, iy, 1)
    col_re = acc[0] * yr - acc[1] * yi
    acc[1] = acc[0] * yi + acc[1] * yr
    acc[0] = col_re
    for part in range(2):
        for x in range(CX):
            four = acc[part, pl.ds(x, 4, stride=CX), :]
            cols[part, x, pl.ds(0, 4), :] = four
            cols[part, x, pl.ds(4, 4), :] = four

    upper = lax.broadcasted_iota(jnp.int32, (8, CY), 0) < 4
    at_once = min(8, total)

    def send_far(k):
        other = lax.rem(me + k, total)
        return pltpu.make_async_remote_copy(
            src_ref=f_send.at[k],
            dst_ref=f_recv.at[k - 1],
            send_sem=f_send_sem,
            recv_sem=f_recv_sem,
            device_id=(lax.div(other, nx), lax.rem(other, nx)),
            device_id_type=MESH,
        )

    def project(trip, carry):
        k0 = trip * at_once
        picked = [bands[lax.rem(me + k0 + j, total)] for j in range(at_once)]

        def pair(rows, part, j):
            return jnp.where(upper, rows.at(part, picked[j], 1), rows.at(part, picked[j + 1], 1))

        pairs = range(0, at_once, 2)
        wr = [pair(cell, 0, j) for j in pairs]
        wi = [pair(cell, 1, j) for j in pairs]
        c_re, c_im = cols[0, CX - 1], cols[1, CX - 1]
        re = [c_re for _ in pairs]
        im = [c_im for _ in pairs]
        for x in range(CX - 2, -1, -1):
            c_re, c_im = cols[0, x], cols[1, x]
            re, im = (
                [r * a - i * b + c_re for r, i, a, b in zip(re, im, wr, wi)],
                [r * b + i * a + c_im for r, i, a, b in zip(re, im, wr, wi)],
            )
        for t, j in enumerate(pairs):
            pr, pi = pair(start_phase, 0, j), pair(start_phase, 1, j)
            far_re = re[t] * pr - im[t] * pi
            far_im = re[t] * pi + im[t] * pr
            f_send[k0 + j] = jnp.where(upper, far_re, pltpu.roll(far_im, 4, 0))
            f_send[k0 + j + 1] = jnp.where(upper, pltpu.roll(far_re, 4, 0), far_im)
        for j in range(at_once):
            @pl.when(k0 + j > 0)
            def _(j=j):
                send_far(k0 + j).start()
        return carry

    lax.fori_loop(0, total // at_once, project, 0)

    for c in range(3):
        for z in range(NZ):
            e_out[c, pl.ds(z * CX, CX), :] = ep[c, at(z), :]
            h_out[c, pl.ds(z * CX, CX), :] = hp[c, at(z), :]

    pltpu.make_async_copy(f_recv, f_recv, f_recv_sem).wait()
    if total <= 64:
        terms = [f_send[0]] + [f_recv[k] for k in range(total - 1)]
        while len(terms) > 1:
            terms = [a + b for a, b in zip(terms[::2], terms[1::2])]
        far_out[...] = terms[0]
    else:
        far_out[...] = lax.fori_loop(0, total - 1, lambda k, t: t + f_recv[k], f_send[0])
    pltpu.make_async_copy(f_recv, f_recv, f_send_sem).wait()


def local(ny, nx, electric, magnetic, material_ids, update_ca, update_cb, face_ranges, band_table):
    total = ny * nx
    bands = band_table.shape[0]
    assert bands == total and electric.shape == (3, NZ, CX, CY)
    scale = 1.0 / math.sqrt(CX * nx * CY * ny)
    f32 = jnp.float32
    vmem = pl.BlockSpec(memory_space=pltpu.VMEM)
    hbm = pl.BlockSpec(memory_space=pltpu.HBM)
    packed, starts = tables(bands, ny)
    rows = NZ * CX
    e_out, h_out, far = pl.pallas_call(
        functools.partial(kernel, ny, nx, scale, starts),
        out_shape=(
            jax.ShapeDtypeStruct((3, rows, CY), f32),
            jax.ShapeDtypeStruct((3, rows, CY), f32),
            jax.ShapeDtypeStruct((8, CY), f32),
        ),
        in_specs=[hbm] * 8,
        out_specs=(vmem, vmem, vmem),
        scratch_shapes=[
            pltpu.VMEM((3, rows, CY), f32),
            pltpu.VMEM((3, rows, CY), f32),
            pltpu.VMEM((rows, CY), jnp.int32),
            pltpu.SMEM((NMAT,), f32),
            pltpu.SMEM((NMAT,), f32),
            pltpu.SMEM((4,), jnp.int32),
            pltpu.SMEM((bands,), jnp.int32),
            pltpu.VMEM(packed.shape, f32),
            pltpu.SemaphoreType.DMA((8,)),
            pltpu.VMEM((3, NZ * PITCH + 8, CY), f32),
            pltpu.VMEM((3, NZ * PITCH + 8, CY), f32),
            pltpu.VMEM((rows, CY), f32),
            pltpu.VMEM((rows, CY), f32),
            pltpu.VMEM((STEPS, 5 * NZ, CY), f32),
            pltpu.VMEM((STEPS, 2 * NZ, CY), f32),
            pltpu.VMEM((STEPS, CX, CY), f32),
            pltpu.VMEM((STEPS, CX, CY), f32),
            pltpu.VMEM((STEPS, 5 * NZ, CY), f32),
            pltpu.VMEM((STEPS, 2 * NZ, CY), f32),
            pltpu.VMEM((STEPS, CX, CY), f32),
            pltpu.VMEM((STEPS, CX, CY), f32),
            pltpu.VMEM((STEPS, NZ, CY), f32),
            pltpu.VMEM((STEPS, 8, CY), f32),
            pltpu.VMEM((4 * CX, CY), f32),
            pltpu.VMEM((2, 4 * CX, CY), f32),
            pltpu.VMEM((2, CX, 8, CY), f32),
            pltpu.VMEM((2 * total, CY), f32),
            pltpu.VMEM((total, 8, CY), f32),
            pltpu.VMEM((total - 1, 8, CY), f32),
            pltpu.SemaphoreType.DMA((6,)),
            pltpu.SemaphoreType.DMA((STEPS, 6)),
            pltpu.SemaphoreType.DMA,
            pltpu.SemaphoreType.DMA,
        ],
        compiler_params=pltpu.CompilerParams(
            collective_id=0, has_side_effects=True, vmem_limit_bytes=62 * 1024 * 1024
        ),
        name="fdtd",
    )(
        electric.reshape(3, rows, CY),
        magnetic.reshape(3, rows, CY),
        material_ids.reshape(rows, CY),
        update_ca,
        update_cb,
        face_ranges.reshape(4),
        band_table,
        packed,
    )
    return (
        e_out.reshape(electric.shape),
        h_out.reshape(electric.shape),
        far.reshape(1, 8, CY),
    )


def solution(mesh):
    in_specs = (
        P(None, None, "inner", "grp"),
        P(None, None, "inner", "grp"),
        P(None, "inner", "grp"),
        P(),
        P(),
        P("inner", "grp", None),
        P(),
    )
    out_specs = (
        P(None, None, "inner", "grp"),
        P(None, None, "inner", "grp"),
        P(("grp", "inner"), None, None),
    )
    body = functools.partial(local, mesh.shape["grp"], mesh.shape["inner"])
    return jax.shard_map(body, mesh=mesh, in_specs=in_specs, out_specs=out_specs, check_vma=False)
```

```python
import functools
import math

import jax
import jax.numpy as jnp
import numpy as np
from jax import lax
from jax.experimental import pallas as pl
from jax.experimental.pallas import tpu as pltpu
from jax.sharding import PartitionSpec as P

STEPS = 8
FREQS = 32
ANG_BAND = 4
NMAT = 8
ZF = 8
NZ = 16
CX = 16
CY = 128
PITCH = 24
BASE = 8
MESH = pl.DeviceIdType.MESH


def tables(bands, groups):
    f = np.tile(np.arange(FREQS, dtype=np.int64) + 1, ANG_BAND)
    b = np.repeat(np.arange(ANG_BAND, dtype=np.int64) * 33 // ANG_BAND - 16, FREQS)
    a = np.arange(bands, dtype=np.int64) - bands // 2

    def both(turns, period):
        angle = (turns % period) * (2.0 * math.pi / period)
        return np.cos(angle).astype(np.float32), np.sin(angle).astype(np.float32)

    y = np.arange(CY, dtype=np.int64)[:, None]
    proj = np.concatenate(both(f * b * y, 4096), axis=1)
    time = np.stack(both(f * np.arange(STEPS, dtype=np.int64)[:, None], 128))
    y_start = np.stack(both(f * b * CY * np.arange(groups, dtype=np.int64)[:, None], 4096))
    cell = np.stack(both(f * a[:, None], 4096))
    block = np.stack(both(f * a[:, None] * CX, 4096))
    flat = [proj[:, :CY], proj[:, CY:]] + [part for table in (time, y_start, cell, block) for part in table]
    starts = np.cumsum([0] + [-(-part.shape[0] // 8) * 8 for part in flat])
    packed = np.zeros((starts[-1], CY), np.float32)
    for start, part in zip(starts, flat):
        packed[start : start + part.shape[0]] = part
    return packed, tuple(int(start) for start in starts[:-1])


class Rows:
    def __init__(self, ref, starts):
        self.ref, self.starts = ref, starts

    def at(self, part, first, count):
        return self.ref[pl.ds(self.starts[part] + first, count), :]


def kernel(
    ny, nx, scale, starts,
    e_hbm, h_hbm, ids_hbm, ca_hbm, cb_hbm, face_hbm, bands_hbm, table_hbm,
    e_out, h_out, far_out,
    e_in, h_in, ids, ca, cb, face, bands, table, in_sem,
    ep, hp, coef_a, coef_b,
    xs_r, xs_l, ys_r, ys_l, xr_l, xr_r, yr_l, yr_r, cor_x, cor_y,
    sample, acc, cols, phase, f_send, f_recv,
    send_sem, recv_sem, f_send_sem, f_recv_sem, hx_send, hx_recv, once_sem,
):
    iy = lax.axis_index("grp")
    ix = lax.axis_index("inner")
    total = ny * nx
    me = iy * nx + ix
    lane = lax.broadcasted_iota(jnp.int32, (CX, CY), 1)
    row = lax.broadcasted_iota(jnp.int32, (CX, CY), 0)

    loads = [
        pltpu.make_async_copy(src, dst, in_sem.at[i])
        for i, (src, dst) in enumerate(
            (
                (e_hbm, e_in),
                (h_hbm, h_in),
                (ids_hbm, ids),
                (ca_hbm, ca),
                (cb_hbm, cb),
                (face_hbm, face),
                (bands_hbm, bands),
                (table_hbm, table),
            )
        )
    ]
    for load in loads:
        load.start()
    time, y_start, cell, block = (Rows(table, starts[i : i + 2]) for i in (2, 4, 6, 8))

    for buf in (hx_recv, xr_l, xr_r, yr_l, yr_r, cor_x, cor_y):
        buf[...] = jnp.zeros(buf.shape, jnp.float32)

    barrier = pltpu.get_barrier_semaphore()

    def greet(k, carry):
        other = lax.rem(me + k, total)
        pl.semaphore_signal(
            barrier, inc=1, device_id=(lax.div(other, nx), lax.rem(other, nx)), device_id_type=MESH
        )
        return carry

    lax.fori_loop(1, total, greet, 0)

    def at(z, shift=0):
        return pl.ds(z * PITCH + BASE + shift, CX)

    def plane(x):
        return pl.ds(BASE + x, NZ, stride=PITCH)

    for c in (1, 2):
        ep[c, plane(CX), :] = jnp.zeros((NZ, CY), jnp.float32)
    for load in loads:
        load.wait()
    for c in range(3):
        for z in range(NZ):
            ep[c, at(z), :] = e_in[c, pl.ds(z * CX, CX), :]
            hp[c, at(z), :] = h_in[c, pl.ds(z * CX, CX), :]
    for z in range(NZ):
        here = ids[pl.ds(z * CX, CX), :]
        va = jnp.zeros((CX, CY), jnp.float32)
        vb = jnp.zeros((CX, CY), jnp.float32)
        for m in range(NMAT):
            chosen = here == m
            va = jnp.where(chosen, ca[m], va)
            vb = jnp.where(chosen, cb[m], vb)
        coef_a[pl.ds(z * CX, CX), :] = va
        coef_b[pl.ds(z * CX, CX), :] = vb
    sample[...] = jnp.zeros(sample.shape, jnp.float32)
    acc[...] = jnp.zeros(acc.shape, jnp.float32)
    on_face = (row >= face[0]) & (row < face[1]) & (lane >= face[2]) & (lane < face[3])
    inside_x = jnp.where(ix > 0, 1.0, 0.0).astype(jnp.float32)
    inside_y = jnp.where(iy > 0, 1.0, 0.0).astype(jnp.float32)

    def power(bit, carry):
        pr, pi, br, bi = carry
        take = lax.rem(lax.shift_right_logical(ix, bit), 2) == 1
        nr = pr * br - pi * bi
        ni = pr * bi + pi * br
        return (
            jnp.where(take, nr, pr),
            jnp.where(take, ni, pi),
            br * br - bi * bi,
            2.0 * br * bi,
        )

    rows_at_once = 8
    for start in range(0, total, rows_at_once):
        part = pl.ds(start, rows_at_once)
        carry = (
            jnp.full((rows_at_once, CY), scale, jnp.float32),
            jnp.zeros((rows_at_once, CY), jnp.float32),
            block.at(0, start, rows_at_once),
            block.at(1, start, rows_at_once),
        )
        for bit in range(max(1, (nx - 1).bit_length())):
            carry = power(bit, carry)
        phase[part, :] = carry[0]
        phase[pl.ds(total + start, rows_at_once), :] = carry[1]

    start_phase = Rows(phase, (0, total))
    pl.semaphore_wait(barrier, total - 1)

    has_xr, has_xl = ix < nx - 1, ix > 0
    has_yr, has_yl = iy < ny - 1, iy > 0

    def copies(n):
        return (
            (has_xr, has_xl, xs_r.at[n], xr_l.at[n], (iy, ix + 1)),
            (has_xl, has_xr, xs_l.at[n], xr_r.at[n], (iy, ix - 1)),
            (has_yr, has_yl, ys_r.at[n], yr_l.at[n], (iy + 1, ix)),
            (has_yl, has_yr, ys_l.at[n], yr_r.at[n], (iy - 1, ix)),
            (has_xr & has_yl, has_xl & has_yr, xs_r.at[n, pl.ds(0, NZ)], cor_x.at[n], (iy - 1, ix + 1)),
            (has_xl & has_yr, has_xr & has_yl, ys_r.at[n, pl.ds(0, 8)], cor_y.at[n], (iy + 1, ix - 1)),
        )

    def remote(n, i, src, dst, device):
        return pltpu.make_async_remote_copy(
            src_ref=src,
            dst_ref=dst,
            send_sem=send_sem.at[i],
            recv_sem=recv_sem.at[n, i],
            device_id=device,
            device_id_type=MESH,
        )

    def start_copies(n, which):
        every = copies(n)
        for i in which:
            sends, _, src, dst, device = every[i]

            @pl.when(sends)
            def _(i=i, src=src, dst=dst, device=device):
                remote(n, i, src, dst, device).start()

    def add_sample(n):
        g_re, g_im = (
            jnp.dot(
                sample[...],
                table[pl.ds(starts[part], CY), :],
                precision=lax.Precision.HIGHEST,
                preferred_element_type=jnp.float32,
            )
            for part in range(2)
        )
        ct, st = time.at(0, n, 1), time.at(1, n, 1)
        acc[0] += ct * g_re + st * g_im
        acc[1] += ct * g_im - st * g_re

    def step(n, carry):
        last = jnp.zeros((CX, CY), jnp.float32)
        first = jnp.zeros((CX, CY), jnp.float32)
        for c in range(3):
            xs_r[n, pl.ds(c * NZ, NZ), :] = ep[c, plane(CX - 1), :]
        for g, c in enumerate((1, 2)):
            xs_l[n, pl.ds(g * NZ, NZ), :] = ep[c, plane(0), :]
        start_copies(n, (4, 0, 1))
        for z in range(NZ):
            for g, (field, c) in enumerate(((ep, 0), (ep, 1), (ep, 2), (hp, 0), (hp, 2))):
                spot = g * NZ + z
                last = jnp.where(lane == spot, pltpu.roll(field[c, at(z), :], (spot - CY + 1) % CY, 1), last)
            for g, c in enumerate((0, 2)):
                spot = g * NZ + z
                value = ep[c, at(z), :]
                first = jnp.where(lane == spot, pltpu.roll(value, spot, 1) if spot else value, first)
        ys_r[n] = last
        ys_l[n] = first
        start_copies(n, (5, 2, 3))

        zero = jnp.zeros((CX, CY), jnp.float32)
        for z in range(NZ):
            ex, ey, ez = (ep[c, at(z), :] for c in range(3))
            ex_z = ep[0, at(z + 1), :] if z < NZ - 1 else zero
            ey_z = ep[1, at(z + 1), :] if z < NZ - 1 else zero
            ey_x = ep[1, at(z, 1), :]
            ez_x = ep[2, at(z, 1), :]
            ex_y = jnp.where(lane == CY - 1, 0.0, pltpu.roll(ex, CY - 1, 1))
            ez_y = jnp.where(lane == CY - 1, 0.0, pltpu.roll(ez, CY - 1, 1))
            hp[0, at(z), :] = hp[0, at(z), :] - 0.5 * ((ez_y - ez) - (ey_z - ey))
            hp[1, at(z), :] = hp[1, at(z), :] - 0.5 * ((ex_z - ex) - (ez_x - ez))
            hp[2, at(z), :] = hp[2, at(z), :] - 0.5 * ((ey_x - ey) - (ex_y - ex))
        add_sample(jnp.maximum(n - 1, 0))

        for i, (_, receives, src, dst, _) in enumerate(copies(n)):
            @pl.when(receives)
            def _(i=i, src=src, dst=dst):
                remote(n, i, src, dst, (iy, ix)).wait_recv()

        @pl.when(n == 0)
        def _():
            @pl.when(has_xl)
            def _():
                once.wait_recv()

            for g, c in enumerate((1, 2)):
                hp[c, plane(-1), :] = hx_recv[pl.ds(g * NZ, NZ), :]

        ex, ey, ez = (xr_l[n, pl.ds(g * NZ, NZ), :] for g in range(3))
        hy, hz = hp[1, plane(-1), :], hp[2, plane(-1), :]
        ey0, ez0 = xs_l[n, pl.ds(0, NZ), :], xs_l[n, pl.ds(NZ, NZ), :]
        hp[1, plane(CX - 1), :] += 0.5 * xr_r[n, pl.ds(NZ, NZ), :]
        hp[2, plane(CX - 1), :] -= 0.5 * xr_r[n, pl.ds(0, NZ), :]
        ex_z = jnp.where(row == NZ - 1, 0.0, pltpu.roll(ex, NZ - 1, 0))
        ex_y = pltpu.roll(jnp.where(lane == 0, cor_x[n], ex), CY - 1, 1)
        hp[1, plane(-1), :] = inside_x * (hy - 0.5 * ((ex_z - ex) - (ez0 - ez)))
        hp[2, plane(-1), :] = inside_x * (hz - 0.5 * ((ey0 - ey) - (ex_y - ex)))

        packed, own = yr_l[n], ys_l[n]
        ex = packed
        ey, ez, hx, hz = (pltpu.roll(packed, CY - g * NZ, 1) for g in range(1, 5))
        ex0, ez0 = own, pltpu.roll(own, CY - NZ, 1)
        ey_z = jnp.where(lane == NZ - 1, 0.0, pltpu.roll(ey, CY - 1, 1))
        corner = pltpu.roll(cor_y[n], CY - NZ, 1)[0:1, :]
        ey_x = jnp.where(row == CX - 1, corner, pltpu.roll(ey, CX - 1, 0))
        hx_col = inside_y * (hx - 0.5 * ((ez0 - ez) - (ey_z - ey)))
        hz_col = inside_y * (hz - 0.5 * ((ey_x - ey) - (ex0 - ex)))

        after = 0.5 * yr_r[n]
        for z in range(NZ):
            hy = hp[1, at(z), :]
            hx = hp[0, at(z), :] - jnp.where(lane == CY - 1, pltpu.roll(after, CY - 1 - NZ - z, 1), 0.0)
            hz = hp[2, at(z), :] + jnp.where(lane == CY - 1, pltpu.roll(after, CY - 1 - z, 1), 0.0)
            hp[0, at(z), :] = hx
            hp[2, at(z), :] = hz
            hx_z = hp[0, at(z - 1), :] if z else zero
            hy_z = hp[1, at(z - 1), :] if z else zero
            hy_x = hp[1, at(z, -1), :]
            hz_x = hp[2, at(z, -1), :]
            hx_y = jnp.where(lane == 0, pltpu.roll(hx_col, CY - z, 1) if z else hx_col, pltpu.roll(hx, 1, 1))
            hz_y = jnp.where(lane == 0, pltpu.roll(hz_col, CY - z, 1) if z else hz_col, pltpu.roll(hz, 1, 1))
            va, vb = coef_a[pl.ds(z * CX, CX), :], coef_b[pl.ds(z * CX, CX), :]
            ex = va * ep[0, at(z), :] + vb * ((hz - hz_y) - (hy - hy_z))
            ey = va * ep[1, at(z), :] + vb * ((hx - hx_z) - (hz - hz_x))
            ep[0, at(z), :] = ex
            ep[1, at(z), :] = ey
            ep[2, at(z), :] = va * ep[2, at(z), :] + vb * ((hy - hy_x) - (hx - hx_y))
            if z == ZF:
                for c, value in enumerate((ex, ey, hx, hy)):
                    sample[pl.ds(c * CX, CX), :] = jnp.where(on_face, value, 0.0)

        for i, (sends, _, src, dst, device) in enumerate(copies(n)):
            @pl.when(sends)
            def _(i=i, src=src, dst=dst, device=device):
                remote(n, i, src, dst, device).wait_send()
        return carry

    once = pltpu.make_async_remote_copy(
        src_ref=hx_send,
        dst_ref=hx_recv,
        send_sem=once_sem.at[0],
        recv_sem=once_sem.at[1],
        device_id=(iy, ix + 1),
        device_id_type=MESH,
    )
    for g, c in enumerate((1, 2)):
        hx_send[pl.ds(g * NZ, NZ), :] = hp[c, plane(CX - 1), :]

    @pl.when(has_xr)
    def _():
        once.start()

    lax.fori_loop(0, STEPS, step, 0)

    @pl.when(has_xr)
    def _():
        once.wait_send()

    add_sample(STEPS - 1)

    yr, yi = y_start.at(0, iy, 1), y_start.at(1, iy, 1)
    col_re = acc[0] * yr - acc[1] * yi
    acc[1] = acc[0] * yi + acc[1] * yr
    acc[0] = col_re
    for part in range(2):
        for x in range(CX):
            four = acc[part, pl.ds(x, 4, stride=CX), :]
            cols[part, x, pl.ds(0, 4), :] = four
            cols[part, x, pl.ds(4, 4), :] = four

    upper = lax.broadcasted_iota(jnp.int32, (8, CY), 0) < 4
    at_once = min(8, total)

    def send_far(k):
        other = lax.rem(me + k, total)
        return pltpu.make_async_remote_copy(
            src_ref=f_send.at[k],
            dst_ref=f_recv.at[k - 1],
            send_sem=f_send_sem,
            recv_sem=f_recv_sem,
            device_id=(lax.div(other, nx), lax.rem(other, nx)),
            device_id_type=MESH,
        )

    def project(trip, carry):
        k0 = trip * at_once
        picked = [bands[lax.rem(me + k0 + j, total)] for j in range(at_once)]

        def pair(rows, part, j):
            return jnp.where(upper, rows.at(part, picked[j], 1), rows.at(part, picked[j + 1], 1))

        pairs = range(0, at_once, 2)
        wr = [pair(cell, 0, j) for j in pairs]
        wi = [pair(cell, 1, j) for j in pairs]
        c_re, c_im = cols[0, CX - 1], cols[1, CX - 1]
        re = [c_re for _ in pairs]
        im = [c_im for _ in pairs]
        for x in range(CX - 2, -1, -1):
            c_re, c_im = cols[0, x], cols[1, x]
            re, im = (
                [r * a - i * b + c_re for r, i, a, b in zip(re, im, wr, wi)],
                [r * b + i * a + c_im for r, i, a, b in zip(re, im, wr, wi)],
            )
        for t, j in enumerate(pairs):
            pr, pi = pair(start_phase, 0, j), pair(start_phase, 1, j)
            far_re = re[t] * pr - im[t] * pi
            far_im = re[t] * pi + im[t] * pr
            f_send[k0 + j] = jnp.where(upper, far_re, pltpu.roll(far_im, 4, 0))
            f_send[k0 + j + 1] = jnp.where(upper, pltpu.roll(far_re, 4, 0), far_im)
        for j in range(at_once):
            @pl.when(k0 + j > 0)
            def _(j=j):
                send_far(k0 + j).start()
        return carry

    lax.fori_loop(0, total // at_once, project, 0)

    for c in range(3):
        for z in range(NZ):
            e_out[c, pl.ds(z * CX, CX), :] = ep[c, at(z), :]
            h_out[c, pl.ds(z * CX, CX), :] = hp[c, at(z), :]

    pltpu.make_async_copy(f_recv, f_recv, f_recv_sem).wait()
    if total <= 64:
        terms = [f_send[0]] + [f_recv[k] for k in range(total - 1)]
        while len(terms) > 1:
            terms = [a + b for a, b in zip(terms[::2], terms[1::2])]
        far_out[...] = terms[0]
    else:
        far_out[...] = lax.fori_loop(0, total - 1, lambda k, t: t + f_recv[k], f_send[0])
    pltpu.make_async_copy(f_recv, f_recv, f_send_sem).wait()


def local(ny, nx, electric, magnetic, material_ids, update_ca, update_cb, face_ranges, band_table):
    total = ny * nx
    bands = band_table.shape[0]
    assert bands == total and electric.shape == (3, NZ, CX, CY)
    scale = 1.0 / math.sqrt(CX * nx * CY * ny)
    f32 = jnp.float32
    vmem = pl.BlockSpec(memory_space=pltpu.VMEM)
    hbm = pl.BlockSpec(memory_space=pltpu.HBM)
    packed, starts = tables(bands, ny)
    rows = NZ * CX
    e_out, h_out, far = pl.pallas_call(
        functools.partial(kernel, ny, nx, scale, starts),
        out_shape=(
            jax.ShapeDtypeStruct((3, rows, CY), f32),
            jax.ShapeDtypeStruct((3, rows, CY), f32),
            jax.ShapeDtypeStruct((8, CY), f32),
        ),
        in_specs=[hbm] * 8,
        out_specs=(vmem, vmem, vmem),
        scratch_shapes=[
            pltpu.VMEM((3, rows, CY), f32),
            pltpu.VMEM((3, rows, CY), f32),
            pltpu.VMEM((rows, CY), jnp.int32),
            pltpu.SMEM((NMAT,), f32),
            pltpu.SMEM((NMAT,), f32),
            pltpu.SMEM((4,), jnp.int32),
            pltpu.SMEM((bands,), jnp.int32),
            pltpu.VMEM(packed.shape, f32),
            pltpu.SemaphoreType.DMA((8,)),
            pltpu.VMEM((3, NZ * PITCH + 8, CY), f32),
            pltpu.VMEM((3, NZ * PITCH + 8, CY), f32),
            pltpu.VMEM((rows, CY), f32),
            pltpu.VMEM((rows, CY), f32),
            pltpu.VMEM((STEPS, 3 * NZ, CY), f32),
            pltpu.VMEM((STEPS, 2 * NZ, CY), f32),
            pltpu.VMEM((STEPS, CX, CY), f32),
            pltpu.VMEM((STEPS, CX, CY), f32),
            pltpu.VMEM((STEPS, 3 * NZ, CY), f32),
            pltpu.VMEM((STEPS, 2 * NZ, CY), f32),
            pltpu.VMEM((STEPS, CX, CY), f32),
            pltpu.VMEM((STEPS, CX, CY), f32),
            pltpu.VMEM((STEPS, NZ, CY), f32),
            pltpu.VMEM((STEPS, 8, CY), f32),
            pltpu.VMEM((4 * CX, CY), f32),
            pltpu.VMEM((2, 4 * CX, CY), f32),
            pltpu.VMEM((2, CX, 8, CY), f32),
            pltpu.VMEM((2 * total, CY), f32),
            pltpu.VMEM((total, 8, CY), f32),
            pltpu.VMEM((total - 1, 8, CY), f32),
            pltpu.SemaphoreType.DMA((6,)),
            pltpu.SemaphoreType.DMA((STEPS, 6)),
            pltpu.SemaphoreType.DMA,
            pltpu.SemaphoreType.DMA,
            pltpu.VMEM((2 * NZ, CY), f32),
            pltpu.VMEM((2 * NZ, CY), f32),
            pltpu.SemaphoreType.DMA((2,)),
        ],
        compiler_params=pltpu.CompilerParams(
            collective_id=0, has_side_effects=True, vmem_limit_bytes=62 * 1024 * 1024
        ),
        name="fdtd",
    )(
        electric.reshape(3, rows, CY),
        magnetic.reshape(3, rows, CY),
        material_ids.reshape(rows, CY),
        update_ca,
        update_cb,
        face_ranges.reshape(4),
        band_table,
        packed,
    )
    return (
        e_out.reshape(electric.shape),
        h_out.reshape(electric.shape),
        far.reshape(1, 8, CY),
    )


def solution(mesh):
    in_specs = (
        P(None, None, "inner", "grp"),
        P(None, None, "inner", "grp"),
        P(None, "inner", "grp"),
        P(),
        P(),
        P("inner", "grp", None),
        P(),
    )
    out_specs = (
        P(None, None, "inner", "grp"),
        P(None, None, "inner", "grp"),
        P(("grp", "inner"), None, None),
    )
    body = functools.partial(local, mesh.shape["grp"], mesh.shape["inner"])
    return jax.shard_map(body, mesh=mesh, in_specs=in_specs, out_specs=out_specs, check_vma=False)
```

```python
import functools
import math

import jax
import jax.numpy as jnp
import numpy as np
from jax import lax
from jax.experimental import pallas as pl
from jax.experimental.pallas import tpu as pltpu
from jax.sharding import PartitionSpec as P

STEPS = 8
FREQS = 32
ANG_BAND = 4
NMAT = 8
ZF = 8
NZ = 16
CX = 16
CY = 128
PITCH = 24
BASE = 8
MESH = pl.DeviceIdType.MESH


def tables(bands, groups):
    f = np.tile(np.arange(FREQS, dtype=np.int64) + 1, ANG_BAND)
    b = np.repeat(np.arange(ANG_BAND, dtype=np.int64) * 33 // ANG_BAND - 16, FREQS)
    a = np.arange(bands, dtype=np.int64) - bands // 2

    def both(turns, period):
        angle = (turns % period) * (2.0 * math.pi / period)
        return np.cos(angle).astype(np.float32), np.sin(angle).astype(np.float32)

    y = np.arange(CY, dtype=np.int64)[:, None]
    proj = np.concatenate(both(f * b * y, 4096), axis=1)
    time = np.stack(both(f * np.arange(STEPS, dtype=np.int64)[:, None], 128))
    y_start = np.stack(both(f * b * CY * np.arange(groups, dtype=np.int64)[:, None], 4096))
    cell = np.stack(both(f * a[:, None], 4096))
    block = np.stack(both(f * a[:, None] * CX, 4096))
    flat = [proj[:, :CY], proj[:, CY:]] + [part for table in (time, y_start, cell, block) for part in table]
    starts = np.cumsum([0] + [-(-part.shape[0] // 8) * 8 for part in flat])
    packed = np.zeros((starts[-1], CY), np.float32)
    for start, part in zip(starts, flat):
        packed[start : start + part.shape[0]] = part
    return packed, tuple(int(start) for start in starts[:-1])


class Rows:
    def __init__(self, ref, starts):
        self.ref, self.starts = ref, starts

    def at(self, part, first, count):
        return self.ref[pl.ds(self.starts[part] + first, count), :]


def kernel(
    ny, nx, scale, starts,
    e_hbm, h_hbm, ids_hbm, ca_hbm, cb_hbm, face_hbm, bands_hbm, table_hbm,
    e_out, h_out, far_out,
    e_in, h_in, ids, ca, cb, face, bands, table, in_sem,
    ep, hp, coef_a, coef_b,
    xs_r, xs_l, ys_r, ys_l, xr_l, xr_r, yr_l, yr_r, cor_x, cor_y,
    sample, acc, cols, phase, f_send, f_recv,
    send_sem, recv_sem, f_send_sem, f_recv_sem, hx_send, hx_recv, once_sem,
):
    iy = lax.axis_index("grp")
    ix = lax.axis_index("inner")
    total = ny * nx
    me = iy * nx + ix
    lane = lax.broadcasted_iota(jnp.int32, (CX, CY), 1)
    row = lax.broadcasted_iota(jnp.int32, (CX, CY), 0)

    loads = [
        pltpu.make_async_copy(src, dst, in_sem.at[i])
        for i, (src, dst) in enumerate(
            (
                (e_hbm, e_in),
                (h_hbm, h_in),
                (ids_hbm, ids),
                (ca_hbm, ca),
                (cb_hbm, cb),
                (face_hbm, face),
                (bands_hbm, bands),
                (table_hbm, table),
            )
        )
    ]
    for load in loads:
        load.start()
    time, y_start, cell, block = (Rows(table, starts[i : i + 2]) for i in (2, 4, 6, 8))

    for buf in (hx_recv, xr_l, xr_r, yr_l, yr_r, cor_x, cor_y):
        buf[...] = jnp.zeros(buf.shape, jnp.float32)

    barrier = pltpu.get_barrier_semaphore()

    def greet(k, carry):
        other = lax.rem(me + k, total)
        pl.semaphore_signal(
            barrier, inc=1, device_id=(lax.div(other, nx), lax.rem(other, nx)), device_id_type=MESH
        )
        return carry

    lax.fori_loop(1, total, greet, 0)

    def at(z, shift=0):
        return pl.ds(z * PITCH + BASE + shift, CX)

    def plane(x):
        return pl.ds(BASE + x, NZ, stride=PITCH)

    for c in (1, 2):
        ep[c, plane(CX), :] = jnp.zeros((NZ, CY), jnp.float32)
    for load in loads:
        load.wait()
    for c in range(3):
        for z in range(NZ):
            ep[c, at(z), :] = e_in[c, pl.ds(z * CX, CX), :]
            hp[c, at(z), :] = h_in[c, pl.ds(z * CX, CX), :]
    for z in range(NZ):
        here = ids[pl.ds(z * CX, CX), :]
        va = jnp.zeros((CX, CY), jnp.float32)
        vb = jnp.zeros((CX, CY), jnp.float32)
        for m in range(NMAT):
            chosen = here == m
            va = jnp.where(chosen, ca[m], va)
            vb = jnp.where(chosen, cb[m], vb)
        coef_a[pl.ds(z * CX, CX), :] = va
        coef_b[pl.ds(z * CX, CX), :] = vb
    sample[...] = jnp.zeros(sample.shape, jnp.float32)
    acc[...] = jnp.zeros(acc.shape, jnp.float32)
    on_face = (row >= face[0]) & (row < face[1]) & (lane >= face[2]) & (lane < face[3])
    inside_x = jnp.where(ix > 0, 1.0, 0.0).astype(jnp.float32)
    inside_y = jnp.where(iy > 0, 1.0, 0.0).astype(jnp.float32)

    def power(bit, carry):
        pr, pi, br, bi = carry
        take = lax.rem(lax.shift_right_logical(ix, bit), 2) == 1
        nr = pr * br - pi * bi
        ni = pr * bi + pi * br
        return (
            jnp.where(take, nr, pr),
            jnp.where(take, ni, pi),
            br * br - bi * bi,
            2.0 * br * bi,
        )

    rows_at_once = 8
    for start in range(0, total, rows_at_once):
        part = pl.ds(start, rows_at_once)
        carry = (
            jnp.full((rows_at_once, CY), scale, jnp.float32),
            jnp.zeros((rows_at_once, CY), jnp.float32),
            block.at(0, start, rows_at_once),
            block.at(1, start, rows_at_once),
        )
        for bit in range(max(1, (nx - 1).bit_length())):
            carry = power(bit, carry)
        phase[part, :] = carry[0]
        phase[pl.ds(total + start, rows_at_once), :] = carry[1]

    start_phase = Rows(phase, (0, total))
    pl.semaphore_wait(barrier, total - 1)

    has_xr, has_xl = ix < nx - 1, ix > 0
    has_yr, has_yl = iy < ny - 1, iy > 0

    def copies(n):
        return (
            (has_xr, has_xl, xs_r.at[n], xr_l.at[n], (iy, ix + 1)),
            (has_xl, has_xr, xs_l.at[n], xr_r.at[n], (iy, ix - 1)),
            (has_yr, has_yl, ys_r.at[n], yr_l.at[n], (iy + 1, ix)),
            (has_yl, has_yr, ys_l.at[n], yr_r.at[n], (iy - 1, ix)),
            (has_xr & has_yl, has_xl & has_yr, xs_r.at[n, pl.ds(0, NZ)], cor_x.at[n], (iy - 1, ix + 1)),
            (has_xl & has_yr, has_xr & has_yl, ys_r.at[n, pl.ds(0, 8)], cor_y.at[n], (iy + 1, ix - 1)),
        )

    def remote(n, i, src, dst, device):
        return pltpu.make_async_remote_copy(
            src_ref=src,
            dst_ref=dst,
            send_sem=send_sem.at[i],
            recv_sem=recv_sem.at[n, i],
            device_id=device,
            device_id_type=MESH,
        )

    def start_copies(n, which):
        every = copies(n)
        for i in which:
            sends, _, src, dst, device = every[i]

            @pl.when(sends)
            def _(i=i, src=src, dst=dst, device=device):
                remote(n, i, src, dst, device).start()

    def add_sample(n):
        g_re, g_im = (
            jnp.dot(
                sample[...],
                table[pl.ds(starts[part], CY), :],
                precision=lax.Precision.HIGHEST,
                preferred_element_type=jnp.float32,
            )
            for part in range(2)
        )
        ct, st = time.at(0, n, 1), time.at(1, n, 1)
        acc[0] += ct * g_re + st * g_im
        acc[1] += ct * g_im - st * g_re

    def step(n, carry):
        last = jnp.zeros((CX, CY), jnp.float32)
        first = jnp.zeros((CX, CY), jnp.float32)
        for c in range(3):
            xs_r[n, pl.ds(c * NZ, NZ), :] = ep[c, plane(CX - 1), :]
        for g, c in enumerate((1, 2)):
            xs_l[n, pl.ds(g * NZ, NZ), :] = ep[c, plane(0), :]
        start_copies(n, (0, 1, 4))
        for z in range(NZ):
            for g, (field, c) in enumerate(((ep, 0), (ep, 1), (ep, 2), (hp, 0), (hp, 2))):
                spot = g * NZ + z
                last = jnp.where(lane == spot, pltpu.roll(field[c, at(z), :], (spot - CY + 1) % CY, 1), last)
            for g, c in enumerate((0, 2)):
                spot = g * NZ + z
                value = ep[c, at(z), :]
                first = jnp.where(lane == spot, pltpu.roll(value, spot, 1) if spot else value, first)
        ys_r[n] = last
        ys_l[n] = first
        start_copies(n, (5, 2, 3))

        zero = jnp.zeros((CX, CY), jnp.float32)
        for z in range(NZ):
            ex, ey, ez = (ep[c, at(z), :] for c in range(3))
            ex_z = ep[0, at(z + 1), :] if z < NZ - 1 else zero
            ey_z = ep[1, at(z + 1), :] if z < NZ - 1 else zero
            ey_x = ep[1, at(z, 1), :]
            ez_x = ep[2, at(z, 1), :]
            ex_y = jnp.where(lane == CY - 1, 0.0, pltpu.roll(ex, CY - 1, 1))
            ez_y = jnp.where(lane == CY - 1, 0.0, pltpu.roll(ez, CY - 1, 1))
            hp[0, at(z), :] = hp[0, at(z), :] - 0.5 * ((ez_y - ez) - (ey_z - ey))
            hp[1, at(z), :] = hp[1, at(z), :] - 0.5 * ((ex_z - ex) - (ez_x - ez))
            hp[2, at(z), :] = hp[2, at(z), :] - 0.5 * ((ey_x - ey) - (ex_y - ex))
        add_sample(jnp.maximum(n - 1, 0))

        for i, (_, receives, src, dst, _) in enumerate(copies(n)):
            @pl.when(receives)
            def _(i=i, src=src, dst=dst):
                remote(n, i, src, dst, (iy, ix)).wait_recv()

        @pl.when(n == 0)
        def _():
            @pl.when(has_xl)
            def _():
                once.wait_recv()

            for g, c in enumerate((1, 2)):
                hp[c, plane(-1), :] = hx_recv[pl.ds(g * NZ, NZ), :]

        ex, ey, ez = (xr_l[n, pl.ds(g * NZ, NZ), :] for g in range(3))
        hy, hz = hp[1, plane(-1), :], hp[2, plane(-1), :]
        ey0, ez0 = xs_l[n, pl.ds(0, NZ), :], xs_l[n, pl.ds(NZ, NZ), :]
        hp[1, plane(CX - 1), :] += 0.5 * xr_r[n, pl.ds(NZ, NZ), :]
        hp[2, plane(CX - 1), :] -= 0.5 * xr_r[n, pl.ds(0, NZ), :]
        ex_z = jnp.where(row == NZ - 1, 0.0, pltpu.roll(ex, NZ - 1, 0))
        ex_y = pltpu.roll(jnp.where(lane == 0, cor_x[n], ex), CY - 1, 1)
        hp[1, plane(-1), :] = inside_x * (hy - 0.5 * ((ex_z - ex) - (ez0 - ez)))
        hp[2, plane(-1), :] = inside_x * (hz - 0.5 * ((ey0 - ey) - (ex_y - ex)))

        packed, own = yr_l[n], ys_l[n]
        ex = packed
        ey, ez, hx, hz = (pltpu.roll(packed, CY - g * NZ, 1) for g in range(1, 5))
        ex0, ez0 = own, pltpu.roll(own, CY - NZ, 1)
        ey_z = jnp.where(lane == NZ - 1, 0.0, pltpu.roll(ey, CY - 1, 1))
        corner = pltpu.roll(cor_y[n], CY - NZ, 1)[0:1, :]
        ey_x = jnp.where(row == CX - 1, corner, pltpu.roll(ey, CX - 1, 0))
        hx_col = inside_y * (hx - 0.5 * ((ez0 - ez) - (ey_z - ey)))
        hz_col = inside_y * (hz - 0.5 * ((ey_x - ey) - (ex0 - ex)))

        after = 0.5 * yr_r[n]
        for z in range(NZ):
            hy = hp[1, at(z), :]
            hx = hp[0, at(z), :] - jnp.where(lane == CY - 1, pltpu.roll(after, CY - 1 - NZ - z, 1), 0.0)
            hz = hp[2, at(z), :] + jnp.where(lane == CY - 1, pltpu.roll(after, CY - 1 - z, 1), 0.0)
            hp[0, at(z), :] = hx
            hp[2, at(z), :] = hz
            hx_z = hp[0, at(z - 1), :] if z else zero
            hy_z = hp[1, at(z - 1), :] if z else zero
            hy_x = hp[1, at(z, -1), :]
            hz_x = hp[2, at(z, -1), :]
            hx_y = jnp.where(lane == 0, pltpu.roll(hx_col, CY - z, 1) if z else hx_col, pltpu.roll(hx, 1, 1))
            hz_y = jnp.where(lane == 0, pltpu.roll(hz_col, CY - z, 1) if z else hz_col, pltpu.roll(hz, 1, 1))
            va, vb = coef_a[pl.ds(z * CX, CX), :], coef_b[pl.ds(z * CX, CX), :]
            ex = va * ep[0, at(z), :] + vb * ((hz - hz_y) - (hy - hy_z))
            ey = va * ep[1, at(z), :] + vb * ((hx - hx_z) - (hz - hz_x))
            ep[0, at(z), :] = ex
            ep[1, at(z), :] = ey
            ep[2, at(z), :] = va * ep[2, at(z), :] + vb * ((hy - hy_x) - (hx - hx_y))
            if z == ZF:
                for c, value in enumerate((ex, ey, hx, hy)):
                    sample[pl.ds(c * CX, CX), :] = jnp.where(on_face, value, 0.0)

        for i, (sends, _, src, dst, device) in enumerate(copies(n)):
            @pl.when(sends)
            def _(i=i, src=src, dst=dst, device=device):
                remote(n, i, src, dst, device).wait_send()
        return carry

    once = pltpu.make_async_remote_copy(
        src_ref=hx_send,
        dst_ref=hx_recv,
        send_sem=once_sem.at[0],
        recv_sem=once_sem.at[1],
        device_id=(iy, ix + 1),
        device_id_type=MESH,
    )
    for g, c in enumerate((1, 2)):
        hx_send[pl.ds(g * NZ, NZ), :] = hp[c, plane(CX - 1), :]

    @pl.when(has_xr)
    def _():
        once.start()

    lax.fori_loop(0, STEPS, step, 0)

    @pl.when(has_xr)
    def _():
        once.wait_send()

    add_sample(STEPS - 1)

    yr, yi = y_start.at(0, iy, 1), y_start.at(1, iy, 1)
    col_re = acc[0] * yr - acc[1] * yi
    acc[1] = acc[0] * yi + acc[1] * yr
    acc[0] = col_re
    for part in range(2):
        for x in range(CX):
            four = acc[part, pl.ds(x, 4, stride=CX), :]
            cols[part, x, pl.ds(0, 4), :] = four
            cols[part, x, pl.ds(4, 4), :] = four

    upper = lax.broadcasted_iota(jnp.int32, (8, CY), 0) < 4
    at_once = min(8, total)

    def send_far(k):
        other = lax.rem(me + k, total)
        return pltpu.make_async_remote_copy(
            src_ref=f_send.at[k],
            dst_ref=f_recv.at[k - 1],
            send_sem=f_send_sem,
            recv_sem=f_recv_sem,
            device_id=(lax.div(other, nx), lax.rem(other, nx)),
            device_id_type=MESH,
        )

    def project(trip, carry):
        k0 = trip * at_once
        picked = [bands[lax.rem(me + k0 + j, total)] for j in range(at_once)]

        def pair(rows, part, j):
            return jnp.where(upper, rows.at(part, picked[j], 1), rows.at(part, picked[j + 1], 1))

        pairs = range(0, at_once, 2)
        wr = [pair(cell, 0, j) for j in pairs]
        wi = [pair(cell, 1, j) for j in pairs]
        c_re, c_im = cols[0, CX - 1], cols[1, CX - 1]
        re = [c_re for _ in pairs]
        im = [c_im for _ in pairs]
        for x in range(CX - 2, -1, -1):
            c_re, c_im = cols[0, x], cols[1, x]
            re, im = (
                [r * a - i * b + c_re for r, i, a, b in zip(re, im, wr, wi)],
                [r * b + i * a + c_im for r, i, a, b in zip(re, im, wr, wi)],
            )
        for t, j in enumerate(pairs):
            pr, pi = pair(start_phase, 0, j), pair(start_phase, 1, j)
            far_re = re[t] * pr - im[t] * pi
            far_im = re[t] * pi + im[t] * pr
            f_send[k0 + j] = jnp.where(upper, far_re, pltpu.roll(far_im, 4, 0))
            f_send[k0 + j + 1] = jnp.where(upper, pltpu.roll(far_re, 4, 0), far_im)
        for j in range(at_once):
            @pl.when(k0 + j > 0)
            def _(j=j):
                send_far(k0 + j).start()
        return carry

    lax.fori_loop(0, total // at_once, project, 0)

    for c in range(3):
        for z in range(NZ):
            e_out[c, pl.ds(z * CX, CX), :] = ep[c, at(z), :]
            h_out[c, pl.ds(z * CX, CX), :] = hp[c, at(z), :]

    pltpu.make_async_copy(f_recv, f_recv, f_recv_sem).wait()
    if total <= 64:
        terms = [f_send[0]] + [f_recv[k] for k in range(total - 1)]
        while len(terms) > 1:
            terms = [a + b for a, b in zip(terms[::2], terms[1::2])]
        far_out[...] = terms[0]
    else:
        far_out[...] = lax.fori_loop(0, total - 1, lambda k, t: t + f_recv[k], f_send[0])
    pltpu.make_async_copy(f_recv, f_recv, f_send_sem).wait()


def local(ny, nx, electric, magnetic, material_ids, update_ca, update_cb, face_ranges, band_table):
    total = ny * nx
    bands = band_table.shape[0]
    assert bands == total and electric.shape == (3, NZ, CX, CY)
    scale = 1.0 / math.sqrt(CX * nx * CY * ny)
    f32 = jnp.float32
    vmem = pl.BlockSpec(memory_space=pltpu.VMEM)
    hbm = pl.BlockSpec(memory_space=pltpu.HBM)
    packed, starts = tables(bands, ny)
    rows = NZ * CX
    e_out, h_out, far = pl.pallas_call(
        functools.partial(kernel, ny, nx, scale, starts),
        out_shape=(
            jax.ShapeDtypeStruct((3, rows, CY), f32),
            jax.ShapeDtypeStruct((3, rows, CY), f32),
            jax.ShapeDtypeStruct((8, CY), f32),
        ),
        in_specs=[hbm] * 8,
        out_specs=(vmem, vmem, vmem),
        scratch_shapes=[
            pltpu.VMEM((3, rows, CY), f32),
            pltpu.VMEM((3, rows, CY), f32),
            pltpu.VMEM((rows, CY), jnp.int32),
            pltpu.SMEM((NMAT,), f32),
            pltpu.SMEM((NMAT,), f32),
            pltpu.SMEM((4,), jnp.int32),
            pltpu.SMEM((bands,), jnp.int32),
            pltpu.VMEM(packed.shape, f32),
            pltpu.SemaphoreType.DMA((8,)),
            pltpu.VMEM((3, NZ * PITCH + 8, CY), f32),
            pltpu.VMEM((3, NZ * PITCH + 8, CY), f32),
            pltpu.VMEM((rows, CY), f32),
            pltpu.VMEM((rows, CY), f32),
            pltpu.VMEM((STEPS, 3 * NZ, CY), f32),
            pltpu.VMEM((STEPS, 2 * NZ, CY), f32),
            pltpu.VMEM((STEPS, CX, CY), f32),
            pltpu.VMEM((STEPS, CX, CY), f32),
            pltpu.VMEM((STEPS, 3 * NZ, CY), f32),
            pltpu.VMEM((STEPS, 2 * NZ, CY), f32),
            pltpu.VMEM((STEPS, CX, CY), f32),
            pltpu.VMEM((STEPS, CX, CY), f32),
            pltpu.VMEM((STEPS, NZ, CY), f32),
            pltpu.VMEM((STEPS, 8, CY), f32),
            pltpu.VMEM((4 * CX, CY), f32),
            pltpu.VMEM((2, 4 * CX, CY), f32),
            pltpu.VMEM((2, CX, 8, CY), f32),
            pltpu.VMEM((2 * total, CY), f32),
            pltpu.VMEM((total, 8, CY), f32),
            pltpu.VMEM((total - 1, 8, CY), f32),
            pltpu.SemaphoreType.DMA((6,)),
            pltpu.SemaphoreType.DMA((STEPS, 6)),
            pltpu.SemaphoreType.DMA,
            pltpu.SemaphoreType.DMA,
            pltpu.VMEM((2 * NZ, CY), f32),
            pltpu.VMEM((2 * NZ, CY), f32),
            pltpu.SemaphoreType.DMA((2,)),
        ],
        compiler_params=pltpu.CompilerParams(
            collective_id=0, has_side_effects=True, vmem_limit_bytes=62 * 1024 * 1024
        ),
        name="fdtd",
    )(
        electric.reshape(3, rows, CY),
        magnetic.reshape(3, rows, CY),
        material_ids.reshape(rows, CY),
        update_ca,
        update_cb,
        face_ranges.reshape(4),
        band_table,
        packed,
    )
    return (
        e_out.reshape(electric.shape),
        h_out.reshape(electric.shape),
        far.reshape(1, 8, CY),
    )


def solution(mesh):
    in_specs = (
        P(None, None, "inner", "grp"),
        P(None, None, "inner", "grp"),
        P(None, "inner", "grp"),
        P(),
        P(),
        P("inner", "grp", None),
        P(),
    )
    out_specs = (
        P(None, None, "inner", "grp"),
        P(None, None, "inner", "grp"),
        P(("grp", "inner"), None, None),
    )
    body = functools.partial(local, mesh.shape["grp"], mesh.shape["inner"])
    return jax.shard_map(body, mesh=mesh, in_specs=in_specs, out_specs=out_specs, check_vma=False)
```
